32 devices in a mesh: parts: 2 (over y), lon: 16 (over z, x, core).
Axes of the slice: x: 2, y: 2, z: 4, core: 2. Of those that a mesh axis runs over, the one named last changes fastest.
Arguments:
- grid_latents: bfloat16 [32768, 512], P(('parts', 'lon')), parts along dimension 0, may hold values from -6 to 6
- mesh_latents: bfloat16 [8192, 512], P(('parts', 'lon')), parts along dimension 0, may hold values from -6 to 6
- send_block: int32 [32, 4], P(('parts', 'lon')), parts along dimension 0, may hold values from 0 to 7
- send_live: int32 [32, 4], P(('parts', 'lon')), parts along dimension 0, may hold values from 0 to 1
- grid_edge_source: int32 [131072], P(('parts', 'lon')), parts along dimension 0, may hold values from 0 to 1535, as said below
- grid_edge_geometry: float32 [4, 131072], P(None, ('parts', 'lon')), parts along dimension 1, may hold values from -1 to 1
- mesh_edge_source: int32 [65536], P(('parts', 'lon')), parts along dimension 0, may hold values from 0 to 895
- mesh_edge_geometry: float32 [4, 65536], P(None, ('parts', 'lon')), parts along dimension 1, may hold values from -1 to 1
- encode_sender: bfloat16 [512, 512], replicated, may hold values from -0.25 to 0.25
- encode_receiver: bfloat16 [512, 512], replicated, may hold values from -0.25 to 0.25
- encode_geometry: float32 [4, 512], replicated, may hold values from -3 to 3
- encode_edge: bfloat16 [512, 512], replicated, may hold values from -0.25 to 0.25
- encode_gather: bfloat16 [512, 512], replicated, may hold values from -0.25 to 0.25
- encode_self: bfloat16 [512, 512], replicated, may hold values from -0.25 to 0.25
- encode_output: bfloat16 [512, 512], replicated, may hold values from -0.25 to 0.25
- process_sender: bfloat16 [2, 512, 512], replicated, may hold values from -0.25 to 0.25
- process_receiver: bfloat16 [2, 512, 512], replicated, may hold values from -0.25 to 0.25
- process_geometry: float32 [2, 4, 512], replicated, may hold values from -3 to 3
- process_edge: bfloat16 [2, 512, 512], replicated, may hold values from -0.25 to 0.25
- process_gather: bfloat16 [2, 512, 512], replicated, may hold values from -0.25 to 0.25
- process_self: bfloat16 [2, 512, 512], replicated, may hold values from -0.25 to 0.25
- process_output: bfloat16 [2, 512, 512], replicated, may hold values from -0.25 to 0.25
Outputs:
- mesh_out: bfloat16 [8192, 512], P(('parts', 'lon')), parts along dimension 0
The draws below stay inside these ranges and needn't reach their ends.
There are 2 independent parts, one for each index of `parts`. The reference program is written for one: setup_inputs(seed, part) draws one part's arguments, and reference() takes and returns one part's arrays. A program takes and returns all parts, laid end to end along the dimension named above; an argument that names none is the same for every part. Nothing has to cross between parts.
Inputs may be any that keep to these rules, and one draw needn't show every extreme that they name: `grid_edge_source`: indices at or above 1024 point into slot k = (index - 1024) // 128 and only where send_live of the sending device (d - o_k) mod 16 is 1 in slot k.
All inputs are finite; a program needn't handle non-finite values.
Results may differ from the reference program's by a relative error of at most 0.012.
Values may be sent and summed in bfloat16 or wider, within the bound.
A program may use at most 64 MiB of HBM per device.

```python
import jax
import jax.numpy as jnp
from jax import lax

D = 512
BLOCK = 128
GB = 8
MESH_DEV = 256
COARSE_DEV = 8
REACH = 2
E_G = 4096
E_M = 2048
STEPS = 2
SLOTS = 4
GRID_DEV = 1024
GRID = 16384
MESH = 4096
EDGES_G = 65536
EDGES_M = 32768
N_LON = 16


def live_table(key):
    key = jax.random.fold_in(key, 11)
    rolled = jax.random.randint(key, (N_LON, SLOTS), 0, 4)
    live = (rolled > 0).astype(jnp.int32)
    rows = jnp.arange(N_LON)[:, None]
    live = jnp.where(rows == 1, 0, live)
    live = jnp.where(rows == REACH, 1, live)
    return live


def draw_send_live(key, part):
    return live_table(key)


def draw_grid_edge_source(key, part):
    live = live_table(key)
    key = jax.random.fold_in(key, 21)
    keys = jax.random.split(key, 4)
    own = jax.random.randint(keys[0], (N_LON, E_G), 0, GRID_DEV)
    slot = jax.random.randint(keys[1], (N_LON, E_G), 0, SLOTS)
    within = jax.random.randint(keys[2], (N_LON, E_G), 0, BLOCK)
    pick = jax.random.randint(keys[3], (N_LON, E_G), 0, 2)
    slots = jnp.arange(SLOTS)
    offsets = (slots // 2 + 1) * (1 - 2 * (slots % 2))
    devices = jnp.arange(N_LON)
    heard = live[(devices[:, None] - offsets[None, :]) % N_LON, slots[None, :]]
    usable = jnp.take_along_axis(heard, slot, axis=1)
    source = jnp.where((pick == 1) & (usable == 1), GRID_DEV + slot * BLOCK + within, own)
    source = source.at[0, 0].set(GRID_DEV + SLOTS * BLOCK - 1).at[0, 1].set(0)
    return source.reshape(-1).astype(jnp.int32)


def draw_mesh_edge_source(key, part):
    key = jax.random.fold_in(key, 31)
    keys = jax.random.split(key, 3)
    nearby = jax.random.randint(keys[0], (N_LON * E_M,), 0, 3 * MESH_DEV)
    distant = 3 * MESH_DEV + jax.random.randint(keys[1], (N_LON * E_M,), 0, N_LON * COARSE_DEV)
    pick = jax.random.randint(keys[2], (N_LON * E_M,), 0, 4)
    source = jnp.where(pick == 0, distant, nearby)
    source = source.at[0].set(3 * MESH_DEV + N_LON * COARSE_DEV - 1).at[1].set(0)
    return source.astype(jnp.int32)


def touch_ends(drawn, rng, least, largest):
    extent = drawn.shape
    spot = [jax.random.randint(jax.random.fold_in(rng, axis), (), 0, extent[axis]) for axis in range(len(extent))]
    drawn = drawn.at[tuple(spot)].set(least)
    longest = extent.index(max(extent))
    spot[longest] = (spot[longest] + 1) % extent[longest]
    return drawn.at[tuple(spot)].set(largest)


def levels(key, extent, cuts, low, top_value):
    gain, own = 1.0, jax.random.fold_in(key, 6)
    for axis_at, shards_of in cuts:
        heights = jnp.exp(jax.random.uniform(jax.random.fold_in(own, axis_at), (shards_of,), jnp.float32, low / len(cuts), top_value / len(cuts)))
        gain = gain * jnp.repeat(heights, extent[axis_at] // shards_of).reshape([-1 if axis == axis_at else 1 for axis in range(len(extent))])
    return gain


def scatter_about(stream_key, dims, scale, most, cuts=(), kind=jnp.bfloat16):
    factor_of = levels(stream_key, dims, cuts, -0.22, 0.18) if cuts else 1.0
    entries = jax.random.normal(stream_key, dims, jnp.float32) * scale * factor_of
    return jnp.minimum(jnp.maximum(entries, -most), most).astype(kind)


def setup_inputs(seed: int = 0, part: int = 0) -> dict:
    arg_keys = jax.random.split(jax.random.key(seed), 23)
    part_splits = jax.random.split(jax.random.fold_in(arg_keys[22], part), 23)
    return {
        "grid_latents": scatter_about(part_splits[0], (GRID, D), 1.0, 6.0, ((0, 16),)),
        "mesh_latents": scatter_about(part_splits[1], (MESH, D), 1.0, 6.0, ((0, 16),)),
        "send_block": touch_ends(jax.random.randint(part_splits[2], (N_LON, SLOTS), 0, GB), jax.random.fold_in(part_splits[2], 1), 0, GB - 1).astype(jnp.int32),
        "send_live": draw_send_live(jax.random.fold_in(jax.random.fold_in(arg_keys[22], part), 71), part),
        "grid_edge_source": draw_grid_edge_source(jax.random.fold_in(jax.random.fold_in(arg_keys[22], part), 71), part),
        "grid_edge_geometry": jnp.clip(jax.random.uniform(part_splits[5], (4, EDGES_G), jnp.float32, -1.0, 1.0) * levels(part_splits[5], (4, EDGES_G), ((1, 16),), -0.4, 0.0), -1.0, 1.0),
        "mesh_edge_source": draw_mesh_edge_source(jax.random.fold_in(jax.random.fold_in(arg_keys[22], part), 71), part),
        "mesh_edge_geometry": jnp.clip(jax.random.uniform(part_splits[7], (4, EDGES_M), jnp.float32, -1.0, 1.0) * levels(part_splits[7], (4, EDGES_M), ((1, 16),), -0.4, 0.0), -1.0, 1.0),
        "encode_sender": scatter_about(arg_keys[8], (D, D), D ** -0.5, 0.25),
        "encode_receiver": scatter_about(arg_keys[9], (D, D), D ** -0.5, 0.25),
        "encode_geometry": scatter_about(arg_keys[10], (4, D), 4 ** -0.5, 3.0, (), jnp.float32),
        "encode_edge": scatter_about(arg_keys[11], (D, D), D ** -0.5, 0.25),
        "encode_gather": scatter_about(arg_keys[12], (D, D), D ** -0.5, 0.25),
        "encode_self": scatter_about(arg_keys[13], (D, D), D ** -0.5, 0.25),
        "encode_output": scatter_about(arg_keys[14], (D, D), D ** -0.5, 0.25),
        "process_sender": scatter_about(arg_keys[15], (STEPS, D, D), D ** -0.5, 0.25),
        "process_receiver": scatter_about(arg_keys[16], (STEPS, D, D), D ** -0.5, 0.25),
        "process_geometry": scatter_about(arg_keys[17], (STEPS, 4, D), 4 ** -0.5, 3.0, (), jnp.float32),
        "process_edge": scatter_about(arg_keys[18], (STEPS, D, D), D ** -0.5, 0.25),
        "process_gather": scatter_about(arg_keys[19], (STEPS, D, D), D ** -0.5, 0.25),
        "process_self": scatter_about(arg_keys[20], (STEPS, D, D), D ** -0.5, 0.25),
        "process_output": scatter_about(arg_keys[21], (STEPS, D, D), D ** -0.5, 0.25),
    }


def layer_norm(values):
    center = lax.optimization_barrier(jnp.mean(values, axis=-1, keepdims=True))
    centred = values - center
    spread = lax.optimization_barrier(jnp.mean(centred * centred, axis=-1, keepdims=True))
    return centred * lax.rsqrt(spread + 1e-05)

def interact(visible, receivers, source, geometry, w_receive, w_geometry, w_edge, w_gather, w_self, w_output):
    node_count, width = receivers.shape
    degree = source.shape[0] // node_count
    pulled = jnp.dot(receivers, w_receive, preferred_element_type=jnp.float32)
    spread_pull = jnp.broadcast_to(pulled[:, None, :], (node_count, degree, width)).reshape(-1, width)
    shape_term = jnp.einsum('ke,kd->ed', geometry, w_geometry, precision=lax.Precision.HIGHEST)
    joined = jax.nn.silu(visible[source].astype(jnp.float32) + spread_pull + shape_term).astype(jnp.bfloat16)
    message = layer_norm(jnp.dot(joined, w_edge, preferred_element_type=jnp.float32)).astype(jnp.bfloat16)
    summed = lax.optimization_barrier(jnp.sum(message.astype(jnp.float32).reshape(node_count, degree, width), axis=1)).astype(jnp.bfloat16)
    update = jax.nn.silu(jnp.dot(summed, w_gather, preferred_element_type=jnp.float32) + jnp.dot(receivers, w_self, preferred_element_type=jnp.float32)).astype(jnp.bfloat16)
    output = layer_norm(jnp.dot(update, w_output, preferred_element_type=jnp.float32))
    return (receivers.astype(jnp.float32) + output).astype(jnp.bfloat16)

def reference(grid_latents, mesh_latents, send_block, send_live, grid_edge_source, grid_edge_geometry, mesh_edge_source, mesh_edge_geometry, encode_sender, encode_receiver, encode_geometry, encode_edge, encode_gather, encode_self, encode_output, process_sender, process_receiver, process_geometry, process_edge, process_gather, process_self, process_output):
    projected = jnp.dot(grid_latents, encode_sender, preferred_element_type=jnp.float32).astype(jnp.bfloat16)
    blocks = projected.reshape(N_LON, GB, BLOCK, D)
    slots = jnp.arange(SLOTS, dtype=jnp.int32)
    offsets = (slots // 2 + 1) * (1 - 2 * (slots % 2))
    devices = jnp.arange(N_LON, dtype=jnp.int32)
    outgoing = blocks[devices[:, None], send_block] * send_live[:, :, None, None].astype(jnp.bfloat16)
    senders = (devices[:, None] - offsets[None, :]) % N_LON
    arrived = outgoing[senders, slots[None, :]]
    own_rows = projected.reshape(N_LON, GRID_DEV, D)
    grid_geometry = grid_edge_geometry.reshape(4, N_LON, E_G).transpose(1, 0, 2)

    def encode_device(pieces):
        own, came, receivers, source, geometry = pieces
        visible = jnp.concatenate([own, came.reshape(SLOTS * BLOCK, D)], axis=0)
        return interact(visible, receivers, source, geometry, encode_receiver, encode_geometry, encode_edge, encode_gather, encode_self, encode_output)
    latents = lax.map(encode_device, (own_rows, arrived, mesh_latents.reshape(N_LON, MESH_DEV, D), grid_edge_source.reshape(N_LON, E_G), grid_geometry))
    mesh_geometry = mesh_edge_geometry.reshape(4, N_LON, E_M).transpose(1, 0, 2)
    mesh_sources = mesh_edge_source.reshape(N_LON, E_M)
    for step in range(STEPS):
        mesh_projected = jnp.dot(latents.reshape(MESH, D), process_sender[step], preferred_element_type=jnp.float32).astype(jnp.bfloat16).reshape(N_LON, MESH_DEV, D)
        before = jnp.roll(mesh_projected, 1, axis=0)
        after = jnp.roll(mesh_projected, -1, axis=0)
        coarse = mesh_projected[:, :COARSE_DEV].reshape(N_LON * COARSE_DEV, D)

        def process_device(pieces, step=step, coarse=coarse):
            left, own, right, receivers, source, geometry = pieces
            visible = jnp.concatenate([left, own, right, coarse], axis=0)
            return interact(visible, receivers, source, geometry, process_receiver[step], process_geometry[step], process_edge[step], process_gather[step], process_self[step], process_output[step])
        latents = lax.map(process_device, (before, mesh_projected, after, latents, mesh_sources, mesh_geometry))
    return latents.reshape(MESH, D)
```

```python
import functools

import jax
import jax.numpy as jnp
from jax import lax
from jax.experimental import pallas as pl
from jax.experimental.pallas import tpu as pltpu
from jax.sharding import PartitionSpec as P

BLOCK = 128
COARSE_DEV = 8
COARSE_ROWS = 16
CHUNK = 64
F32 = jnp.float32
BF16 = jnp.bfloat16


def dot(a, b):
    return jnp.dot(a, b, preferred_element_type=F32)


def silu(v):
    half = 0.5 * v
    return half + half * jnp.tanh(half)


def layer_norm(v):
    centred = v - jnp.mean(v, axis=-1, keepdims=True)
    spread = jnp.mean(centred * centred, axis=-1, keepdims=True)
    return centred * lax.rsqrt(spread + 1e-05)


def node_chunk(
    rows, n, degree, visible, meta_ref, at_index, at_geometry, hot, pulled, own_term, receivers,
    w_geometry, w_edge, w_gather, w_output,
):
    width = pulled.shape[1]
    depth = visible.shape[0]
    meta = meta_ref[rows, :]
    lane = lax.broadcasted_iota(jnp.int32, (n, 128), 1).astype(F32)
    for j in range(degree):
        away = jnp.broadcast_to(meta[:, at_index + j : at_index + j + 1], (n, 128)) - lane
        for tile in range(depth // 128):
            hot[j * n : (j + 1) * n, tile * 128 : (tile + 1) * 128] = jnp.where(
                away == float(tile * 128), 1.0, 0.0
            ).astype(BF16)
    picked = dot(hot[: degree * n, :depth], visible[...])
    base = pulled[rows, :]
    w_g = w_geometry[...]
    joined = []
    for j in range(degree):
        term = picked[j * n : (j + 1) * n] + base
        for k in range(4):
            col = at_geometry + k * degree + j
            term = term + meta[:, col : col + 1] * w_g[k : k + 1, :]
        joined.append(silu(term).astype(BF16))
    message = layer_norm(dot(jnp.concatenate(joined, axis=0), w_edge[...]))
    message = message.astype(BF16).astype(F32)
    summed = message[:n]
    for j in range(1, degree):
        summed = summed + message[j * n : (j + 1) * n]
    update = silu(dot(summed.astype(BF16), w_gather[...]) + own_term[rows, :]).astype(BF16)
    out = layer_norm(dot(update, w_output[...]))
    return (receivers[rows, :].astype(F32) + out).astype(BF16)


def kernel(
    peers, steps, degrees,
    chosen, meta_in, grid_in, mesh_in, *rest,
):
    weights_in = rest[:14]
    out_ref = rest[14]
    (meta, grid, mesh_lat, *weights) = rest[15 : 15 + 17]
    (
        visible, outgoing, mesh_visible, latents, pulled, own_term, hot,
        load_sem, slot_send, slot_recv, near_send, near_recv, far_send, far_recv,
    ) = rest[32:]
    (
        e_sender, e_receiver, e_geometry, e_edge, e_gather, e_self, e_output,
        p_sender, p_receiver, p_geometry, p_edge, p_gather, p_self, p_output,
    ) = weights
    me = lax.axis_index("lon")
    slots = outgoing.shape[0] // BLOCK
    offsets = [(s // 2 + 1) * (1 - 2 * (s % 2)) for s in range(slots)]
    nodes = mesh_lat.shape[0]
    grid_rows = grid.shape[0]
    chunks = nodes // CHUNK

    def peer(by):
        return lax.rem(me + by + peers, peers)

    barrier = pltpu.get_barrier_semaphore()

    def greet(by, carry):
        pl.semaphore_signal(
            barrier, inc=1, device_id={"lon": peer(by)}, device_id_type=pl.DeviceIdType.MESH
        )
        return carry

    lax.fori_loop(1, peers, greet, 0)

    loads = {}
    pairs = {"grid": (grid_in, grid), "meta": (meta_in, meta), "mesh": (mesh_in, mesh_lat)}
    for at in range(14):
        pairs[at] = (weights_in[at], weights[at])
    order = ["grid", 0, "mesh", 1, 5, "meta", 2, 3, 4, 6, 7, 8, 12, 9, 10, 11, 13]
    for at, name in enumerate(order):
        loads[name] = pltpu.make_async_copy(*pairs[name], load_sem.at[at])
        loads[name].start()

    loads["grid"].wait()
    loads[0].wait()
    w_sender = e_sender[...]
    for s in range(slots):
        total = None
        for b in range(grid_rows // BLOCK):
            part = grid[b * BLOCK : (b + 1) * BLOCK, :].astype(F32) * chosen[0, s, b]
            total = part if total is None else total + part
        outgoing[s * BLOCK : (s + 1) * BLOCK, :] = dot(total.astype(BF16), w_sender).astype(BF16)
    pl.semaphore_wait(barrier, peers - 1)
    slot_copies = []
    for s in range(slots):
        copy = pltpu.make_async_remote_copy(
            src_ref=outgoing.at[pl.ds(s * BLOCK, BLOCK)],
            dst_ref=visible.at[pl.ds(grid_rows + s * BLOCK, BLOCK)],
            send_sem=slot_send.at[s],
            recv_sem=slot_recv.at[s],
            device_id={"lon": peer(offsets[s])},
            device_id_type=pl.DeviceIdType.MESH,
        )
        copy.start()
        slot_copies.append(copy)
    visible[:grid_rows, :] = dot(grid[...], w_sender).astype(BF16)
    loads["mesh"].wait()
    loads[1].wait()
    pulled[...] = dot(mesh_lat[...], e_receiver[...])
    loads[5].wait()
    own_term[...] = dot(mesh_lat[...], e_self[...])
    for name in ("meta", 2, 3, 4, 6, 7):
        loads[name].wait()
    for copy in slot_copies:
        copy.wait()

    def near_copy(step, chunk, side):
        landing = 0 if side == 0 else 2 * nodes
        start = pl.multiple_of(chunk * CHUNK, CHUNK)
        return pltpu.make_async_remote_copy(
            src_ref=mesh_visible.at[step, pl.ds(nodes + start, CHUNK)],
            dst_ref=mesh_visible.at[step, pl.ds(landing + start, CHUNK)],
            send_sem=near_send.at[step, side, chunk],
            recv_sem=near_recv.at[step, side, chunk],
            device_id={"lon": peer(1 if side == 0 else -1)},
            device_id_type=pl.DeviceIdType.MESH,
        )

    def far_copy(step, by, sender):
        start = pl.multiple_of(3 * nodes + sender * COARSE_ROWS, COARSE_ROWS)
        return pltpu.make_async_remote_copy(
            src_ref=mesh_visible.at[step, pl.ds(nodes, COARSE_ROWS)],
            dst_ref=mesh_visible.at[step, pl.ds(start, COARSE_ROWS)],
            send_sem=far_send.at[step, by],
            recv_sem=far_recv.at[step, sender],
            device_id={"lon": peer(by)},
            device_id_type=pl.DeviceIdType.MESH,
        )

    def hand_on(step, chunk, fresh):
        start = pl.multiple_of(chunk * CHUNK, CHUNK)
        latents[step, pl.ds(start, CHUNK), :] = fresh
        ours = dot(fresh, p_sender[step]).astype(BF16)
        mesh_visible[step, pl.ds(nodes + start, CHUNK), :] = ours

        @pl.when(chunk == 0)
        def _():
            at = pl.multiple_of(3 * nodes + me * COARSE_ROWS, COARSE_ROWS)
            mesh_visible[step, pl.ds(at, COARSE_ROWS), :] = ours[:COARSE_ROWS]

            def send(by, carry):
                far_copy(step, by, me).start()
                return carry

            lax.fori_loop(1, peers, send, 0)

        for side in range(2):
            near_copy(step, chunk, side).start()

    def encode(chunk, carry):
        rows = pl.ds(pl.multiple_of(chunk * CHUNK, CHUNK), CHUNK)
        fresh = node_chunk(
            rows, CHUNK, degrees[0], visible, meta, 0, degrees[0] + degrees[1], hot, pulled,
            own_term, mesh_lat, e_geometry, e_edge, e_gather, e_output,
        )
        hand_on(0, chunk, fresh)
        return carry

    lax.fori_loop(0, chunks, encode, 0)

    for name in (8, 12, 9, 10, 11, 13):
        loads[name].wait()
    for step in range(steps):
        pulled[...] = dot(latents[step], p_receiver[step])
        own_term[...] = dot(latents[step], p_self[step])

        def settle_near(chunk, carry):
            for side in range(2):
                near_copy(step, chunk, side).wait()
            return carry

        lax.fori_loop(0, chunks, settle_near, 0)

        def settle_far(by, carry):
            far_copy(step, by, me).wait_send()
            far_copy(step, by, peer(-by)).wait_recv()
            return carry

        lax.fori_loop(1, peers, settle_far, 0)

        def process(chunk, carry):
            rows = pl.ds(pl.multiple_of(chunk * CHUNK, CHUNK), CHUNK)
            fresh = node_chunk(
                rows, CHUNK, degrees[1], mesh_visible.at[step], meta, degrees[0],
                5 * degrees[0] + degrees[1], hot, pulled, own_term, latents.at[step],
                p_geometry.at[step], p_edge.at[step], p_gather.at[step], p_output.at[step],
            )
            if step + 1 < steps:
                hand_on(step + 1, chunk, fresh)
            else:
                out_ref[rows, :] = fresh
            return carry

        lax.fori_loop(0, chunks, process, 0)


def local(
    grid_latents, mesh_latents, send_block, send_live, grid_edge_source, grid_edge_geometry,
    mesh_edge_source, mesh_edge_geometry, *weights,
):
    peers = lax.axis_size("lon")
    width = grid_latents.shape[1]
    nodes = mesh_latents.shape[0]
    slots = send_block.shape[1]
    steps = weights[7].shape[0]
    degrees = (grid_edge_source.shape[0] // nodes, mesh_edge_source.shape[0] // nodes)
    far = mesh_edge_source - 3 * nodes
    placed = jnp.where(
        far < 0,
        mesh_edge_source,
        3 * nodes + (far // COARSE_DEV) * COARSE_ROWS + far % COARSE_DEV,
    )
    meta = jnp.concatenate(
        [
            grid_edge_source.reshape(nodes, -1).astype(F32),
            placed.reshape(nodes, -1).astype(F32),
        ]
        + [grid_edge_geometry[k].reshape(nodes, -1) for k in range(4)]
        + [mesh_edge_geometry[k].reshape(nodes, -1) for k in range(4)],
        axis=1,
    )
    meta = jnp.pad(meta, ((0, 0), (0, -meta.shape[1] % 128)))
    table = 3 * nodes + peers * COARSE_ROWS
    grid_rows = grid_latents.shape[0]
    chunks = nodes // CHUNK
    deepest = max(grid_rows + slots * BLOCK, table)
    chosen = (send_block[:, :, None] == jnp.arange(grid_rows // BLOCK)) * send_live[:, :, None]
    held = [meta, grid_latents, mesh_latents, *weights]
    return pl.pallas_call(
        functools.partial(kernel, peers, steps, degrees),
        out_shape=jax.ShapeDtypeStruct(mesh_latents.shape, BF16),
        in_specs=[pl.BlockSpec(memory_space=pltpu.SMEM)]
        + [pl.BlockSpec(memory_space=pl.ANY)] * 17,
        out_specs=pl.BlockSpec(memory_space=pltpu.VMEM),
        scratch_shapes=[pltpu.VMEM(a.shape, a.dtype) for a in held]
        + [
            pltpu.VMEM((grid_rows + slots * BLOCK, width), BF16),
            pltpu.VMEM((slots * BLOCK, width), BF16),
            pltpu.VMEM((steps, table, width), BF16),
            pltpu.VMEM((steps, nodes, width), BF16),
            pltpu.VMEM((nodes, width), F32),
            pltpu.VMEM((nodes, width), F32),
            pltpu.VMEM((CHUNK * max(degrees), deepest), BF16),
            pltpu.SemaphoreType.DMA((17,)),
            pltpu.SemaphoreType.DMA((slots,)),
            pltpu.SemaphoreType.DMA((slots,)),
            pltpu.SemaphoreType.DMA((steps, 2, chunks)),
            pltpu.SemaphoreType.DMA((steps, 2, chunks)),
            pltpu.SemaphoreType.DMA((steps, peers)),
            pltpu.SemaphoreType.DMA((steps, peers)),
        ],
        compiler_params=pltpu.CompilerParams(
            collective_id=0, has_side_effects=True, vmem_limit_bytes=56 * 1024 * 1024
        ),
    )(chosen.astype(F32), *held)


def solution(mesh):
    spread = P(("parts", "lon"), None)
    placed = (
        spread, spread, spread, spread,
        P(("parts", "lon")), P(None, ("parts", "lon")),
        P(("parts", "lon")), P(None, ("parts", "lon")),
    ) + (P(),) * 14
    return jax.shard_map(
        local, mesh=mesh, in_specs=placed, out_specs=spread, check_vma=False
    )
```

```python
import functools

import jax
import jax.numpy as jnp
from jax import lax
from jax.experimental import pallas as pl
from jax.experimental.pallas import tpu as pltpu
from jax.sharding import PartitionSpec as P

BLOCK = 128
COARSE_DEV = 8
COARSE_ROWS = 16
F32 = jnp.float32
BF16 = jnp.bfloat16


def dot(a, b):
    return jnp.dot(a, b, preferred_element_type=F32)


def silu(v):
    half = 0.5 * v
    return half + half * jnp.tanh(half)


def layer_norm(v):
    centred = v - jnp.mean(v, axis=-1, keepdims=True)
    spread = jnp.mean(centred * centred, axis=-1, keepdims=True)
    return centred * lax.rsqrt(spread + 1e-05)


PARTS = 3


def one_hot(index_ref, rows, n, degree, first, depth, hot):
    index = index_ref[rows, :]
    lane = lax.broadcasted_iota(jnp.int32, (n, 128), 1) + first
    for j in range(degree):
        away = (jnp.broadcast_to(index[:, j : j + 1], (n, 128)) - lane).astype(jnp.int16)
        for tile in range(depth // 128):
            hot[j * n : (j + 1) * n, tile * 128 : (tile + 1) * 128] = jnp.where(
                away == jnp.int16(tile * 128), jnp.array(1, BF16), jnp.array(0, BF16)
            )


def geometry_rows(w_geometry, degree, depth):
    w = w_geometry[...]
    high = w.astype(BF16).astype(F32)
    rows = [
        jnp.broadcast_to(part[k : k + 1], (degree, w.shape[1]))
        for part in (high, high, w - high)
        for k in range(4)
    ]
    rows.append(jnp.zeros((depth - PARTS * 4 * degree, w.shape[1]), F32))
    return jnp.concatenate(rows, axis=0).astype(BF16)


def geometry_columns(geometry_ref, rows, n, degree, at, hot):
    value = geometry_ref[rows, :]
    depth = value.shape[1]
    lane = lax.broadcasted_iota(jnp.int32, value.shape, 1)
    high = value.astype(BF16).astype(F32)
    part = jnp.where((lane >= 4 * degree) & (lane < 8 * degree), value - high, high)
    turn = lane % degree
    for j in range(degree):
        hot[j * n : (j + 1) * n, at : at + depth] = jnp.where(turn == j, part, 0.0).astype(BF16)


def pick_early(rows, n, degree, table, first_geometry, index_ref, geometry_ref, hot, picked, chunk):
    depth = geometry_ref.shape[1]
    one_hot(index_ref, rows, n, degree, 0, first_geometry, hot)
    geometry_columns(geometry_ref, rows, n, degree, first_geometry, hot)
    width = first_geometry + depth
    picked[pl.ds(pl.multiple_of(chunk * n * degree, 128), n * degree), :] = dot(
        hot[: n * degree, :width], table[:width, :]
    )


def node_chunk(
    rows, n, degree, table, late, index_ref, hot, picked, chunk, pulled, own_term, receivers,
    w_edge, w_gather, w_output,
):
    depth = table.shape[0] - late
    one_hot(index_ref, rows, n, degree, late, depth, hot)
    term = picked[pl.ds(pl.multiple_of(chunk * n * degree, 128), n * degree), :]
    term = term + dot(hot[: degree * n, :depth], table[late:, :])
    base = pulled[rows, :]
    joined = [silu(term[j * n : (j + 1) * n] + base).astype(BF16) for j in range(degree)]
    message = layer_norm(dot(jnp.concatenate(joined, axis=0), w_edge[...]))
    summed = message[:n]
    for j in range(1, degree):
        summed = summed + message[j * n : (j + 1) * n]
    update = silu(dot(summed.astype(BF16), w_gather[...]) + own_term[rows, :]).astype(BF16)
    out = layer_norm(dot(update, w_output[...]))
    return (receivers[rows, :].astype(F32) + out).astype(BF16)


def kernel(
    peers, steps, degrees,
    chosen, index_g_in, index_m_in, geometry_g_in, geometry_m_in, grid_in, mesh_in, *rest,
):
    weights_in = rest[:14]
    out_ref = rest[14]
    (index_g, index_m, geometry_g, geometry_m, grid, mesh_lat, *weights) = rest[15 : 15 + 20]
    (
        visible, outgoing, mesh_visible, latents, pulled, own_term, hot, picked,
        load_sem, slot_send, slot_recv, near_send, near_recv, far_send, far_recv,
    ) = rest[35:]
    (
        e_sender, e_receiver, e_geometry, e_edge, e_gather, e_self, e_output,
        p_sender, p_receiver, p_geometry, p_edge, p_gather, p_self, p_output,
    ) = weights
    me = lax.axis_index("lon")
    slots = outgoing.shape[0] // BLOCK
    offsets = [(s // 2 + 1) * (1 - 2 * (s % 2)) for s in range(slots)]
    nodes = mesh_lat.shape[0]
    grid_rows = grid.shape[0]
    chunks = 2
    half = nodes // chunks
    degree_g, degree_m = degrees
    slot_base = grid_rows + geometry_g.shape[1]
    far_base = 2 * nodes
    geometry_base = far_base + peers * COARSE_ROWS
    late_base = geometry_base + geometry_m.shape[1]

    def peer(by):
        return lax.rem(me + by + peers, peers)

    barrier = pltpu.get_barrier_semaphore()

    def greet(by, carry):
        pl.semaphore_signal(
            barrier, inc=1, device_id={"lon": peer(by)}, device_id_type=pl.DeviceIdType.MESH
        )
        return carry

    lax.fori_loop(1, peers, greet, 0)

    loads = {}
    pairs = {"grid": (grid_in, grid), "mesh": (mesh_in, mesh_lat)}
    pairs["ig"] = (index_g_in, index_g)
    pairs["im"] = (index_m_in, index_m)
    pairs["gg"] = (geometry_g_in, geometry_g)
    pairs["gm"] = (geometry_m_in, geometry_m)
    for at in range(14):
        pairs[at] = (weights_in[at], weights[at])
    order = ["grid", 0, "mesh", 1, 5, 2, "ig", "gg", 3, 4, 6, 7, 9, 8, 12, "im", "gm", 10, 11, 13]
    for at, name in enumerate(order):
        loads[name] = pltpu.make_async_copy(*pairs[name], load_sem.at[at])
        loads[name].start()

    loads["grid"].wait()
    loads[0].wait()
    w_sender = e_sender[...]
    for s in range(slots):
        total = None
        for b in range(grid_rows // BLOCK):
            part = grid[b * BLOCK : (b + 1) * BLOCK, :].astype(F32) * chosen[0, s, b]
            total = part if total is None else total + part
        outgoing[s * BLOCK : (s + 1) * BLOCK, :] = dot(total.astype(BF16), w_sender).astype(BF16)
    pl.semaphore_wait(barrier, peers - 1)
    slot_copies = []
    for s in range(slots):
        copy = pltpu.make_async_remote_copy(
            src_ref=outgoing.at[pl.ds(s * BLOCK, BLOCK)],
            dst_ref=visible.at[pl.ds(slot_base + s * BLOCK, BLOCK)],
            send_sem=slot_send.at[s],
            recv_sem=slot_recv.at[s],
            device_id={"lon": peer(offsets[s])},
            device_id_type=pl.DeviceIdType.MESH,
        )
        copy.start()
        slot_copies.append(copy)
    visible[:grid_rows, :] = dot(grid[...], w_sender).astype(BF16)
    loads["mesh"].wait()
    loads[1].wait()
    pulled[...] = dot(mesh_lat[...], e_receiver[...])
    loads[5].wait()
    own_term[...] = dot(mesh_lat[...], e_self[...])
    for name in (2, "ig", "gg"):
        loads[name].wait()
    visible[grid_rows:slot_base, :] = geometry_rows(e_geometry, degree_g, slot_base - grid_rows)

    def rows_of(chunk):
        return pl.ds(pl.multiple_of(chunk * half, half), half)

    def early_g(chunk, carry):
        pick_early(
            rows_of(chunk), half, degree_g, visible, grid_rows, index_g, geometry_g, hot, picked, chunk
        )
        return carry

    lax.fori_loop(0, chunks, early_g, 0)
    for name in (3, 4, 6, 7, 9):
        loads[name].wait()
    for copy in slot_copies:
        copy.wait()

    def near_copy(step, chunk, side):
        landing = (nodes if chunk == 0 else late_base) + side * half
        return pltpu.make_async_remote_copy(
            src_ref=mesh_visible.at[step, pl.ds(chunk * half, half)],
            dst_ref=mesh_visible.at[step, pl.ds(landing, half)],
            send_sem=near_send.at[step, side, chunk],
            recv_sem=near_recv.at[step, side, chunk],
            device_id={"lon": peer(1 if side == 0 else -1)},
            device_id_type=pl.DeviceIdType.MESH,
        )

    def far_copy(step, by, sender):
        start = pl.multiple_of(far_base + sender * COARSE_ROWS, COARSE_ROWS)
        return pltpu.make_async_remote_copy(
            src_ref=mesh_visible.at[step, pl.ds(0, COARSE_ROWS)],
            dst_ref=mesh_visible.at[step, pl.ds(start, COARSE_ROWS)],
            send_sem=far_send.at[step, by],
            recv_sem=far_recv.at[step, sender],
            device_id={"lon": peer(by)},
            device_id_type=pl.DeviceIdType.MESH,
        )

    def hand_on(step, chunk, fresh):
        rows = rows_of(chunk)
        latents[step, rows, :] = fresh
        ours = dot(fresh, p_sender[step]).astype(BF16)
        mesh_visible[step, rows, :] = ours

        @pl.when(chunk == 0)
        def _():
            for side in range(2):
                near_copy(step, 0, side).start()
            at = pl.multiple_of(far_base + me * COARSE_ROWS, COARSE_ROWS)
            mesh_visible[step, pl.ds(at, COARSE_ROWS), :] = ours[:COARSE_ROWS]

            def send(by, carry):
                far_copy(step, by, me).start()
                return carry

            lax.fori_loop(1, peers, send, 0)

        @pl.when(chunk == 1)
        def _():
            for side in range(2):
                near_copy(step, 1, side).start()

    def encode(chunk, carry):
        fresh = node_chunk(
            rows_of(chunk), half, degree_g, visible, slot_base, index_g, hot, picked, chunk, pulled,
            own_term, mesh_lat, e_edge, e_gather, e_output,
        )
        hand_on(0, chunk, fresh)
        return carry

    lax.fori_loop(0, chunks, encode, 0)

    for name in (8, 12, "im", "gm", 10, 11, 13):
        loads[name].wait()
    for step in range(steps):
        table = mesh_visible.at[step]
        pulled[...] = dot(latents[step], p_receiver[step])
        own_term[...] = dot(latents[step], p_self[step])
        table[geometry_base:late_base, :] = geometry_rows(
            p_geometry.at[step], degree_m, late_base - geometry_base
        )
        for side in range(2):
            near_copy(step, 0, side).wait()

        def settle_far(by, carry):
            far_copy(step, by, me).wait_send()
            far_copy(step, by, peer(-by)).wait_recv()
            return carry

        lax.fori_loop(1, peers, settle_far, 0)

        def early_m(chunk, carry):
            pick_early(
                rows_of(chunk), half, degree_m, table, geometry_base, index_m, geometry_m, hot,
                picked, chunk,
            )
            return carry

        lax.fori_loop(0, chunks, early_m, 0)
        for side in range(2):
            near_copy(step, 1, side).wait()

        def process(chunk, carry):
            fresh = node_chunk(
                rows_of(chunk), half, degree_m, table, late_base, index_m, hot, picked, chunk,
                pulled, own_term, latents.at[step], p_edge.at[step], p_gather.at[step],
                p_output.at[step],
            )
            if step + 1 < steps:
                hand_on(step + 1, chunk, fresh)
            else:
                out_ref[rows_of(chunk), :] = fresh
            return carry

        lax.fori_loop(0, chunks, process, 0)


def spread_geometry(geometry, nodes, degree):
    flat = geometry.reshape(4, nodes, degree).transpose(1, 0, 2).reshape(nodes, 4 * degree)
    blank = jnp.zeros((nodes, -PARTS * 4 * degree % 128), F32)
    return jnp.concatenate([flat] * PARTS + [blank], axis=1)


def local(
    grid_latents, mesh_latents, send_block, send_live, grid_edge_source, grid_edge_geometry,
    mesh_edge_source, mesh_edge_geometry, *weights,
):
    peers = lax.axis_size("lon")
    width = grid_latents.shape[1]
    nodes = mesh_latents.shape[0]
    slots = send_block.shape[1]
    steps = weights[7].shape[0]
    degrees = (grid_edge_source.shape[0] // nodes, mesh_edge_source.shape[0] // nodes)
    grid_rows = grid_latents.shape[0]
    geometry_g = spread_geometry(grid_edge_geometry, nodes, degrees[0])
    geometry_m = spread_geometry(mesh_edge_geometry, nodes, degrees[1])
    index_g = jnp.where(
        grid_edge_source < grid_rows, grid_edge_source, grid_edge_source + geometry_g.shape[1]
    ).reshape(nodes, -1)
    half = nodes // 2
    far_base = 2 * nodes
    late_base = far_base + peers * COARSE_ROWS + geometry_m.shape[1]
    part, within = mesh_edge_source // nodes, mesh_edge_source % nodes
    beside = jnp.where(within < half, nodes + within, late_base + within - half)
    beside = jnp.where(part == 2, beside + half, beside)
    far = mesh_edge_source - 3 * nodes
    index_m = jnp.where(
        part == 1,
        within,
        jnp.where(
            part < 3, beside, far_base + (far // COARSE_DEV) * COARSE_ROWS + far % COARSE_DEV
        ),
    ).reshape(nodes, -1)
    table_g = grid_rows + geometry_g.shape[1] + slots * BLOCK
    table_m = late_base + nodes
    chunks = 2
    chosen = (send_block[:, :, None] == jnp.arange(grid_rows // BLOCK)) * send_live[:, :, None]
    held = [index_g, index_m, geometry_g, geometry_m, grid_latents, mesh_latents, *weights]
    return pl.pallas_call(
        functools.partial(kernel, peers, steps, degrees),
        out_shape=jax.ShapeDtypeStruct(mesh_latents.shape, BF16),
        in_specs=[pl.BlockSpec(memory_space=pltpu.SMEM)]
        + [pl.BlockSpec(memory_space=pl.ANY)] * 20,
        out_specs=pl.BlockSpec(memory_space=pltpu.VMEM),
        scratch_shapes=[pltpu.VMEM(a.shape, a.dtype) for a in held]
        + [
            pltpu.VMEM((table_g, width), BF16),
            pltpu.VMEM((slots * BLOCK, width), BF16),
            pltpu.VMEM((steps, table_m, width), BF16),
            pltpu.VMEM((steps, nodes, width), BF16),
            pltpu.VMEM((nodes, width), F32),
            pltpu.VMEM((nodes, width), F32),
            pltpu.VMEM((half * max(degrees), max(table_g, table_m)), BF16),
            pltpu.VMEM((nodes * max(degrees), width), F32),
            pltpu.SemaphoreType.DMA((20,)),
            pltpu.SemaphoreType.DMA((slots,)),
            pltpu.SemaphoreType.DMA((slots,)),
            pltpu.SemaphoreType.DMA((steps, 2, chunks)),
            pltpu.SemaphoreType.DMA((steps, 2, chunks)),
            pltpu.SemaphoreType.DMA((steps, peers)),
            pltpu.SemaphoreType.DMA((steps, peers)),
        ],
        compiler_params=pltpu.CompilerParams(
            collective_id=0, has_side_effects=True, vmem_limit_bytes=56 * 1024 * 1024
        ),
    )(chosen.astype(F32), *held)


def solution(mesh):
    spread = P(("parts", "lon"), None)
    placed = (
        spread, spread, spread, spread,
        P(("parts", "lon")), P(None, ("parts", "lon")),
        P(("parts", "lon")), P(None, ("parts", "lon")),
    ) + (P(),) * 14
    return jax.shard_map(
        local, mesh=mesh, in_specs=placed, out_specs=spread, check_vma=False
    )
```
